32 devices in a mesh: dp: 2 (over x), row: 4 (over y, core), col: 4 (over z).
Axes of the slice: x: 2, y: 2, z: 4, core: 2. Of those that a mesh axis runs over, the one named last changes fastest.
Arguments:
- tokens: bfloat16 [512, 6144], P(('dp', 'col'), 'row'), may hold values from -6 to 6
- grad_out: bfloat16 [512, 6144], P(('dp', 'col'), 'row'), may hold values from -6 to 6
- w_in: bfloat16 [6144, 24576], P('row', 'col'), may hold values from -0.078125 to 0.078125
- w_out: bfloat16 [24576, 6144], P('col', 'row'), may hold values from -0.0390625 to 0.0390625
Outputs:
- output: bfloat16 [512, 6144], P(('dp', 'col'), 'row')
- grad_tokens: bfloat16 [512, 6144], P(('dp', 'col'), 'row')
- grad_w_in: bfloat16 [6144, 24576], P('row', 'col')
- grad_w_out: bfloat16 [24576, 6144], P('col', 'row')
The draws below stay inside these ranges and needn't reach their ends.
All inputs are finite; a program needn't handle non-finite values.
Results may differ from the reference program's by a relative error of at most 0.03.
Values may be sent and summed in bfloat16 or wider, within the bound.
A program may use at most 192 MiB of HBM per device.

```python
import jax
import jax.numpy as jnp
from jax import lax

D = 6144
FF = 24576
GROUP_TOK = 256
TOKENS = 512
N_DP = 2
N_ROW = 4


def steps_of(key, shape, shards, low, largest):
    def one(dim, parts):
        steps = jax.random.uniform(jax.random.fold_in(jax.random.fold_in(key, 6), dim), (parts,), jnp.float32, low / len(shards), largest / len(shards))
        return jnp.repeat(jnp.exp(steps), shape[dim] // parts).reshape((-1,) + (1,) * (len(shape) - dim - 1))

    factor_of = one(*shards[0])
    for cut in shards[1:]:
        factor_of = factor_of * one(*cut)
    return factor_of


def centred(stream_key, dims, scale, bound, shards=(), dtype=jnp.bfloat16):
    result = jax.random.normal(stream_key, dims, jnp.float32) * scale
    if len(shards) > 0:
        result = steps_of(stream_key, dims, shards, -0.22, 0.18) * result
    return jnp.clip(result, min=-bound, max=bound).astype(dtype)


def setup_inputs(seed: int = 0) -> dict:
    key_of = jax.random.split(jax.random.key(seed), 5)
    tokens = centred(key_of[0], (TOKENS, D), 1.0, 6.0, ((0, 8), (1, 4)))
    grad_out = centred(key_of[1], (TOKENS, D), 1.0, 6.0, ((0, 8), (1, 4)))
    w_in = centred(key_of[2], (D, FF), D ** -0.5, 0.078125, ((0, 4), (1, 4)))
    w_out = centred(key_of[3], (FF, D), FF ** -0.5, 0.0390625, ((0, 4), (1, 4)))
    return dict(tokens=tokens, grad_out=grad_out, w_in=w_in, w_out=w_out)


def gelu_tanh(value):
    return jax.nn.gelu(value, approximate=True)

def rounded(value):
    return lax.optimization_barrier(value.astype(jnp.bfloat16)).astype(jnp.float32)

def reference(tokens, grad_out, w_in, w_out):
    width = D // N_ROW
    outputs = []
    grads = []
    acc_in = jnp.zeros((D, FF), jnp.float32)
    acc_out = jnp.zeros((FF, D), jnp.float32)
    for group in range(N_DP):
        x_rows = tokens[group * GROUP_TOK:(group + 1) * GROUP_TOK]
        dy_rows = grad_out[group * GROUP_TOK:(group + 1) * GROUP_TOK]
        pre = jnp.zeros((GROUP_TOK, FF), jnp.float32)
        grad_hidden = jnp.zeros((GROUP_TOK, FF), jnp.float32)
        for block in range(N_ROW):
            lo = block * width
            hi = lo + width
            pre = pre + rounded(jnp.dot(x_rows[:, lo:hi], w_in[lo:hi], preferred_element_type=jnp.float32))
            grad_hidden = grad_hidden + rounded(lax.dot_general(dy_rows[:, lo:hi], w_out[:, lo:hi], (((1,), (1,)), ((), ())), preferred_element_type=jnp.float32))
        hidden = gelu_tanh(pre).astype(jnp.bfloat16)
        _, pullback = jax.vjp(gelu_tanh, pre)
        grad_pre = pullback(grad_hidden)[0].astype(jnp.bfloat16)
        outputs.append(jnp.dot(hidden, w_out, preferred_element_type=jnp.float32).astype(jnp.bfloat16))
        grads.append(lax.dot_general(grad_pre, w_in, (((1,), (1,)), ((), ())), preferred_element_type=jnp.float32).astype(jnp.bfloat16))
        acc_in = acc_in + rounded(lax.dot_general(x_rows, grad_pre, (((0,), (0,)), ((), ())), preferred_element_type=jnp.float32))
        acc_out = acc_out + rounded(lax.dot_general(hidden, dy_rows, (((0,), (0,)), ((), ())), preferred_element_type=jnp.float32))
    output = jnp.concatenate(outputs, axis=0)
    grad_tokens = jnp.concatenate(grads, axis=0)
    return (output, grad_tokens, acc_in.astype(jnp.bfloat16), acc_out.astype(jnp.bfloat16))
```

```python
import jax
import jax.numpy as jnp
from jax import lax
from jax.sharding import PartitionSpec as P


def gelu_tanh(value):
    return jax.nn.gelu(value, approximate=True)


def gelu_back(pre, grad_hidden):
    _, pullback = jax.vjp(gelu_tanh, pre)
    return pullback(grad_hidden)[0].astype(jnp.bfloat16)


def contract_rows(left, right):
    return lax.dot_general(
        left, right, (((0,), (0,)), ((), ())), preferred_element_type=jnp.float32
    )


def contract_cols(left, right):
    return lax.dot_general(
        left, right, (((1,), (1,)), ((), ())), preferred_element_type=jnp.float32
    )


def gather(value, axis):
    return lax.all_gather(value, axis, axis=0, tiled=True)


def swap(value):
    return lax.ppermute(value, "dp", [(0, 1), (1, 0)])


def scatter(value, axis):
    return lax.psum_scatter(value, axis, scatter_dimension=0, tiled=True)


def shards(tokens, grad_out, w_in, w_out):
    group_x, group_dy = gather(tokens, "col"), gather(grad_out, "col")
    other_x, other_dy = swap(group_x), swap(group_dy)
    pre_part = jnp.dot(group_x, w_in, preferred_element_type=jnp.float32)
    pre_share = scatter(pre_part.astype(jnp.bfloat16), "row").astype(jnp.float32)
    grad_part = contract_cols(group_dy, w_out)
    grad_share = scatter(grad_part.astype(jnp.bfloat16), "row").astype(jnp.float32)
    hidden_share = gelu_tanh(pre_share).astype(jnp.bfloat16)
    grad_pre_share = gelu_back(pre_share, grad_share)
    hidden, grad_pre = gather(hidden_share, "row"), gather(grad_pre_share, "row")
    other_hidden = gather(swap(hidden_share), "row")
    other_grad_pre = gather(swap(grad_pre_share), "row")
    out_part = jnp.dot(hidden, w_out, preferred_element_type=jnp.float32)
    output = scatter(out_part.astype(jnp.bfloat16), "col")
    back_part = contract_cols(grad_pre, w_in)
    grad_tokens = scatter(back_part.astype(jnp.bfloat16), "col")
    both_x = jnp.concatenate([group_x, other_x], axis=0)
    both_dy = jnp.concatenate([group_dy, other_dy], axis=0)
    both_hidden = jnp.concatenate([hidden, other_hidden], axis=0)
    both_grad_pre = jnp.concatenate([grad_pre, other_grad_pre], axis=0)
    total_out = contract_rows(both_hidden, both_dy).astype(jnp.bfloat16)
    total_in = contract_rows(both_x, both_grad_pre).astype(jnp.bfloat16)
    return output, grad_tokens, total_in, total_out


def solution(mesh):
    specs = (
        P(("dp", "col"), "row"),
        P(("dp", "col"), "row"),
        P("row", "col"),
        P("col", "row"),
    )
    return jax.shard_map(
        shards, mesh=mesh, in_specs=specs, out_specs=specs, check_vma=False
    )
```

```python
import functools
import math

import jax
import jax.numpy as jnp
from jax import lax
from jax.experimental import pallas as pl
from jax.experimental.pallas import tpu as pltpu
from jax.sharding import PartitionSpec as P

MESH = pl.DeviceIdType.MESH
F32 = jnp.float32
BF16 = jnp.bfloat16
SCALE = math.sqrt(2.0 / math.pi)
CUBIC = 0.044715


def contract_rows(left, right):
    return lax.dot_general(
        left, right, (((0,), (0,)), ((), ())), preferred_element_type=F32
    )


def contract_cols(left, right):
    return lax.dot_general(
        left, right, (((1,), (1,)), ((), ())), preferred_element_type=F32
    )


def tile_of(size, largest):
    tile = largest
    while size % tile:
        tile -= 128
    return tile


def middle(
    sizes,
    x_ref, dy_ref, w_in, w_out,
    out_ref, back_ref, hid_all, gp_all, x_all, dy_all,
    xg, parts, crecv, ysend, yrecv, gat, wa_in, wa_out, we_in, we_out,
    acc_out, acc_back,
    x_local, x_ssem, x_rsem, d_ssem, d_rsem,
    c_ssem, c_rsem, y_ssem, y_rsem, ag_rsem, ag_y, ag_x, ag_c,
    wa_sem, we_sem, o_sem, xo_sem,
):
    n_col, n_y, chunks, width = sizes
    rows, depth = x_ref.shape
    group = rows * n_col
    share = group // (2 * n_y)
    me_dp, me_row, me_col = (lax.axis_index(a) for a in ("dp", "row", "col"))
    me_y, me_k = me_row // 2, me_row % 2
    other_dp, other_k = 1 - me_dp, 1 - me_k

    def y_peer(d):
        return lax.rem(me_y + d, n_y)

    def y_from(d):
        return lax.rem(me_y + n_y - d, n_y)

    def col_peer(d):
        return lax.rem(me_col + d, n_col)

    def col_from(d):
        return lax.rem(me_col + n_col - d, n_col)

    def remote(src, dst, ssem, rsem, peer):
        return pltpu.make_async_remote_copy(
            src_ref=src, dst_ref=dst, send_sem=ssem, recv_sem=rsem,
            device_id=peer, device_id_type=MESH,
        )

    to_core = {"row": me_y * 2 + other_k}
    to_dp = {"dp": other_dp}

    barrier = pltpu.get_barrier_semaphore()
    peers = [to_core, to_dp]
    peers += [{"row": y_peer(d) * 2 + me_k} for d in range(1, n_y)]
    peers += [{"col": col_peer(d)} for d in range(1, n_col)]
    for peer in peers:
        pl.semaphore_signal(barrier, inc=1, device_id=peer, device_id_type=MESH)

    def load_a(c, slot):
        cols = pl.ds(pl.multiple_of(c * width, width), width)
        return (
            pltpu.make_async_copy(w_in.at[:, cols], wa_in.at[slot], wa_sem.at[slot, 0]),
            pltpu.make_async_copy(w_out.at[cols, :], wa_out.at[slot], wa_sem.at[slot, 1]),
        )

    def load_e(c, slot):
        cols = pl.ds(pl.multiple_of(c * width, width), width)
        return (
            pltpu.make_async_copy(w_in.at[:, cols], we_in.at[slot], we_sem.at[slot, 0]),
            pltpu.make_async_copy(w_out.at[cols, :], we_out.at[slot], we_sem.at[slot, 1]),
        )

    for copy in load_a(0, 0):
        copy.start()
    own = [
        pltpu.make_async_copy(ref, xg.at[a, me_dp, me_col], x_local.at[a])
        for a, ref in enumerate((x_ref, dy_ref))
    ]
    for copy in own:
        copy.start()
    acc_out[...] = jnp.zeros_like(acc_out)
    acc_back[...] = jnp.zeros_like(acc_back)
    pl.semaphore_wait(barrier, len(peers))

    def x_copy(a, d, at):
        ref = (x_ref, dy_ref)[a]
        return remote(
            ref, xg.at[a, me_dp, at], x_ssem.at[a, d - 1], x_rsem.at[a, d - 1],
            {"col": col_peer(d)},
        )

    for a in range(2):
        for d in range(1, n_col):
            x_copy(a, d, me_col).start()
    for copy in own:
        copy.wait()
    for a in range(2):
        for d in range(1, n_col):
            x_copy(a, d, col_from(d)).wait_recv()

    def d_copy(a, dp):
        return remote(xg.at[a, dp], xg.at[a, dp], d_ssem.at[a], d_rsem.at[a], to_dp)

    for a in range(2):
        d_copy(a, me_dp).start()

    def core_copy(c, k):
        return remote(parts.at[c, k], crecv.at[c], c_ssem.at[c], c_rsem.at[c], to_core)

    def y_copy(c, d):
        return remote(
            ysend.at[c, d - 1], yrecv.at[c, d - 1], y_ssem.at[c, d - 1],
            y_rsem.at[c, d - 1], {"row": y_peer(d) * 2 + me_k},
        )

    def piece(c, dp, y, k):
        return gat.at[c, :, dp, y, k]

    def share_copy(c, dp, y, k, ssem, peer):
        ref = piece(c, dp, y, k)
        return remote(ref, ref, ssem, ag_rsem.at[c, dp, y, k], peer)

    def ag_y_copy(c, d, y):
        return share_copy(c, me_dp, y, me_k, ag_y.at[c, d - 1], {"row": y_peer(d) * 2 + me_k})

    def ag_x_copy(c, dp, y):
        return share_copy(c, dp, y, me_k, ag_x.at[c, y], to_dp)

    def ag_c_copy(c, dp, y, k):
        return share_copy(c, dp, y, k, ag_c.at[c, dp, y], to_core)

    def out_copy(c, a):
        cols = pl.ds(pl.multiple_of(c * width, width), width)
        return pltpu.make_async_copy(
            gat.at[c, a], (hid_all, gp_all)[a].at[:, :, :, :, cols], o_sem.at[c, a]
        )

    n_tile = tile_of(width, 256)
    d_tile = tile_of(depth, 256)

    def stage_a(c):
        slot = lax.rem(c, 2)

        @pl.when(c + 1 < chunks)
        def _():
            for copy in load_a(c + 1, 1 - slot):
                copy.start()

        for copy in load_a(c, slot):
            copy.wait()
        x = xg[0, me_dp].reshape(group, depth)
        dy = xg[1, me_dp].reshape(group, depth)
        for t in range(width // n_tile):
            cols = slice(t * n_tile, (t + 1) * n_tile)
            pre = jnp.dot(x, wa_in[slot, :, cols], preferred_element_type=F32)
            grad = contract_cols(dy, wa_out[slot, cols, :])
            for a, part in enumerate((pre, grad)):
                part = part.astype(BF16)
                for r in range(2 * n_y):
                    parts[c, r % 2, a, r // 2, :, cols] = part[r * share:(r + 1) * share]
        core_copy(c, other_k).start()

    def stage_b(c):
        core_copy(c, me_k).wait_recv()
        for d in range(1, n_y):
            y = y_peer(d)
            for a in range(2):
                ysend[c, d - 1, a] = (
                    parts[c, me_k, a, y].astype(F32) + crecv[c, a, y].astype(F32)
                ).astype(BF16)
            y_copy(c, d).start()

    def stage_c(c):
        for d in range(1, n_y):
            y_copy(c, d).wait_recv()
        for t in range(width // n_tile):
            cols = slice(t * n_tile, (t + 1) * n_tile)

            def total(a):
                value = parts[c, me_k, a, me_y, :, cols].astype(F32)
                value = value + crecv[c, a, me_y, :, cols].astype(F32)
                for d in range(1, n_y):
                    value = value + yrecv[c, d - 1, a, :, cols].astype(F32)
                return value

            pre, grad = total(0), total(1)
            square = pre * pre
            bend = jnp.tanh(SCALE * (pre + CUBIC * (square * pre)))
            half = 0.5 * (1.0 + bend)
            slope = half + (0.5 * pre) * (1.0 - bend * bend) * (
                SCALE * (1.0 + (3.0 * CUBIC) * square)
            )
            gat[c, 0, me_dp, me_y, me_k, :, cols] = (pre * half).astype(BF16)
            gat[c, 1, me_dp, me_y, me_k, :, cols] = (grad * slope).astype(BF16)
        for d in range(1, n_y):
            ag_y_copy(c, d, me_y).start()
        ag_x_copy(c, me_dp, me_y).start()
        ag_c_copy(c, me_dp, me_y, me_k).start()

    def stage_d(c):
        for d in range(1, n_y):
            y = y_from(d)
            ag_y_copy(c, d, y).wait_recv()
            ag_c_copy(c, me_dp, y, me_k).start()
            ag_x_copy(c, me_dp, y).start()

    def stage_e(c):
        slot = lax.rem(c, 2)

        @pl.when(c + 1 < chunks)
        def _():
            for copy in load_e(c + 1, 1 - slot):
                copy.start()

        for y in range(n_y):
            ag_c_copy(c, me_dp, y, other_k).wait_recv()
        for copy in load_e(c, slot):
            copy.wait()
        hidden = gat[c, 0, me_dp].reshape(group, width)
        grad_pre = gat[c, 1, me_dp].reshape(group, width)
        for t in range(depth // d_tile):
            cols = slice(t * d_tile, (t + 1) * d_tile)
            acc_out[:, cols] += jnp.dot(
                hidden, we_out[slot, :, cols], preferred_element_type=F32
            )
            acc_back[:, cols] += contract_cols(grad_pre, we_in[slot, cols, :])
        for y in range(n_y):
            ag_x_copy(c, other_dp, y).wait_recv()
            ag_c_copy(c, other_dp, y, me_k).start()

    def stage_f(c):
        for y in range(n_y):
            ag_c_copy(c, other_dp, y, other_k).wait_recv()
        for a in range(2):
            out_copy(c, a).start()

    def step(i, carry):
        @pl.when(i == 1)
        def _():
            for copy in load_e(0, 0):
                copy.start()

        for lag, stage in enumerate((stage_a, stage_b, stage_c, stage_d, stage_e, stage_f)):
            @pl.when(jnp.logical_and(i >= lag, i < chunks + lag))
            def _(lag=lag, stage=stage):
                stage(i - lag)

        return carry

    lax.fori_loop(0, chunks + 5, step, 0)

    out_ref[...] = acc_out[...].astype(BF16)
    back_ref[...] = acc_back[...].astype(BF16)
    x_out = []
    for a in range(2):
        d_copy(a, other_dp).wait_recv()
        x_out.append(pltpu.make_async_copy(xg.at[a], (x_all, dy_all)[a], xo_sem.at[a]))
        x_out[a].start()
    for a in range(2):
        d_copy(a, me_dp).wait_send()
        for d in range(1, n_col):
            x_copy(a, d, me_col).wait_send()

    def drain(c, carry):
        core_copy(c, other_k).wait_send()
        for d in range(1, n_y):
            y_copy(c, d).wait_send()
            ag_y_copy(c, d, me_y).wait_send()
        for y in range(n_y):
            ag_x_copy(c, me_dp, y).wait_send()
            for dp in range(2):
                ag_c_copy(c, dp, y, me_k).wait_send()
        for a in range(2):
            out_copy(c, a).wait()
        return carry

    lax.fori_loop(0, chunks, drain, 0)
    for copy in x_out:
        copy.wait()


def shards(mesh, tokens, grad_out, w_in, w_out):
    n_col, n_y = mesh.shape["col"], mesh.shape["row"] // 2
    rows, depth = tokens.shape
    hidden_units = w_in.shape[1]
    group = rows * n_col
    share = group // (2 * n_y)
    width = tile_of(hidden_units, 768)
    chunks = hidden_units // width
    dma = pltpu.SemaphoreType.DMA
    vmem, any_space = pl.BlockSpec(memory_space=pltpu.VMEM), pl.BlockSpec(memory_space=pl.ANY)
    shape = jax.ShapeDtypeStruct
    out_part, back_part, hid, gp, x_all, dy_all = pl.pallas_call(
        functools.partial(middle, (n_col, n_y, chunks, width)),
        out_shape=(
            shape((group, depth), BF16),
            shape((group, depth), BF16),
            shape((2, n_y, 2, share, hidden_units), BF16),
            shape((2, n_y, 2, share, hidden_units), BF16),
            shape((2, n_col, rows, depth), BF16),
            shape((2, n_col, rows, depth), BF16),
        ),
        in_specs=[vmem, vmem, any_space, any_space],
        out_specs=[vmem, vmem] + [any_space] * 4,
        scratch_shapes=[
            pltpu.VMEM((2, 2, n_col, rows, depth), BF16),
            pltpu.VMEM((chunks, 2, 2, n_y, share, width), BF16),
            pltpu.VMEM((chunks, 2, n_y, share, width), BF16),
            pltpu.VMEM((chunks, n_y - 1, 2, share, width), BF16),
            pltpu.VMEM((chunks, n_y - 1, 2, share, width), BF16),
            pltpu.VMEM((chunks, 2, 2, n_y, 2, share, width), BF16),
            pltpu.VMEM((2, depth, width), BF16),
            pltpu.VMEM((2, width, depth), BF16),
            pltpu.VMEM((2, depth, width), BF16),
            pltpu.VMEM((2, width, depth), BF16),
            pltpu.VMEM((group, depth), F32),
            pltpu.VMEM((group, depth), F32),
            dma((2,)),
            dma((2, n_col - 1)),
            dma((2, n_col - 1)),
            dma((2,)),
            dma((2,)),
            dma((chunks,)),
            dma((chunks,)),
            dma((chunks, n_y - 1)),
            dma((chunks, n_y - 1)),
            dma((chunks, 2, n_y, 2)),
            dma((chunks, n_y - 1)),
            dma((chunks, n_y)),
            dma((chunks, 2, n_y)),
            dma((2, 2)),
            dma((2, 2)),
            dma((chunks, 2)),
            dma((2,)),
        ],
        compiler_params=pltpu.CompilerParams(
            collective_id=0, has_side_effects=True, vmem_limit_bytes=60 * 2**20
        ),
        cost_estimate=pl.CostEstimate(
            flops=8 * group * depth * hidden_units,
            bytes_accessed=8 * depth * hidden_units,
            transcendentals=0,
        ),
        name="middle",
    )(tokens, grad_out, w_in, w_out)
    output = lax.psum_scatter(out_part, "col", scatter_dimension=0, tiled=True)
    grad_tokens = lax.psum_scatter(back_part, "col", scatter_dimension=0, tiled=True)
    both = 2 * group
    grad_w_out = contract_rows(
        hid.reshape(both, hidden_units), dy_all.reshape(both, depth)
    ).astype(BF16)
    grad_w_in = contract_rows(
        x_all.reshape(both, depth), gp.reshape(both, hidden_units)
    ).astype(BF16)
    return output, grad_tokens, grad_w_in, grad_w_out


def solution(mesh):
    specs = (
        P(("dp", "col"), "row"),
        P(("dp", "col"), "row"),
        P("row", "col"),
        P("col", "row"),
    )
    return jax.shard_map(
        functools.partial(shards, mesh),
        mesh=mesh, in_specs=specs, out_specs=specs, check_vma=False,
    )
```

```python
import functools
import math

import jax
import jax.numpy as jnp
from jax import lax
from jax.experimental import pallas as pl
from jax.experimental.pallas import tpu as pltpu
from jax.sharding import PartitionSpec as P

MESH = pl.DeviceIdType.MESH
F32 = jnp.float32
BF16 = jnp.bfloat16
SCALE = math.sqrt(2.0 / math.pi)
CUBIC = 0.044715


def contract_rows(left, right):
    return lax.dot_general(
        left, right, (((0,), (0,)), ((), ())), preferred_element_type=F32
    )


def contract_cols(left, right):
    return lax.dot_general(
        left, right, (((1,), (1,)), ((), ())), preferred_element_type=F32
    )


def tile_of(size, largest):
    tile = largest
    while size % tile:
        tile -= 128
    return tile


def middle(
    sizes,
    x_ref, dy_ref, w_in, w_out,
    out_ref, hid_all, gp_all, x_all, dy_all,
    xg, parts, crecv, ysend, yrecv, gat, wa_in, wa_out, we_in, we_out,
    acc_out, acc_back,
    x_local, x_ssem, x_rsem, d_ssem, d_rsem,
    c_ssem, c_rsem, y_ssem, y_rsem, ag_rsem, ag_y, ag_x, ag_c,
    wa_sem, we_sem, o_sem, xo_sem,
):
    n_col, n_y, chunks, width = sizes
    rows, depth = x_ref.shape
    group = rows * n_col
    share = group // (2 * n_y)
    me_dp, me_row, me_col = (lax.axis_index(a) for a in ("dp", "row", "col"))
    me_y, me_k = me_row // 2, me_row % 2
    other_dp, other_k = 1 - me_dp, 1 - me_k

    def y_peer(d):
        return lax.rem(me_y + d, n_y)

    def y_from(d):
        return lax.rem(me_y + n_y - d, n_y)

    def col_peer(d):
        return lax.rem(me_col + d, n_col)

    def col_from(d):
        return lax.rem(me_col + n_col - d, n_col)

    def remote(src, dst, ssem, rsem, peer):
        return pltpu.make_async_remote_copy(
            src_ref=src, dst_ref=dst, send_sem=ssem, recv_sem=rsem,
            device_id=peer, device_id_type=MESH,
        )

    to_core = {"row": me_y * 2 + other_k}
    to_dp = {"dp": other_dp}

    barrier = pltpu.get_barrier_semaphore()
    peers = [to_core, to_dp]
    peers += [{"row": y_peer(d) * 2 + me_k} for d in range(1, n_y)]
    peers += [{"col": col_peer(d)} for d in range(1, n_col)]
    for peer in peers:
        pl.semaphore_signal(barrier, inc=1, device_id=peer, device_id_type=MESH)

    def load_a(c, slot):
        cols = pl.ds(pl.multiple_of(c * width, width), width)
        return (
            pltpu.make_async_copy(w_in.at[:, cols], wa_in.at[slot], wa_sem.at[slot, 0]),
            pltpu.make_async_copy(w_out.at[cols, :], wa_out.at[slot], wa_sem.at[slot, 1]),
        )

    def load_e(c, slot):
        cols = pl.ds(pl.multiple_of(c * width, width), width)
        return (
            pltpu.make_async_copy(w_in.at[:, cols], we_in.at[slot], we_sem.at[slot, 0]),
            pltpu.make_async_copy(w_out.at[cols, :], we_out.at[slot], we_sem.at[slot, 1]),
        )

    for copy in load_a(0, 0):
        copy.start()
    own = [
        pltpu.make_async_copy(ref, xg.at[a, me_dp, me_col], x_local.at[a])
        for a, ref in enumerate((x_ref, dy_ref))
    ]
    for copy in own:
        copy.start()
    acc_out[...] = jnp.zeros_like(acc_out)
    acc_back[...] = jnp.zeros_like(acc_back)
    pl.semaphore_wait(barrier, len(peers))

    def x_copy(a, d, at):
        ref = (x_ref, dy_ref)[a]
        return remote(
            ref, xg.at[a, me_dp, at], x_ssem.at[a, d - 1], x_rsem.at[a, d - 1],
            {"col": col_peer(d)},
        )

    for a in range(2):
        for d in range(1, n_col):
            x_copy(a, d, me_col).start()
    for copy in own:
        copy.wait()

    def d_copy(a, dp, d):
        ref = xg.at[a, dp, col_from(d)]
        return remote(ref, ref, d_ssem.at[a, d], d_rsem.at[a, d], to_dp)

    for a in range(2):
        d_copy(a, me_dp, 0).start()
    for a in range(2):
        for d in range(1, n_col):
            x_copy(a, d, col_from(d)).wait_recv()
            d_copy(a, me_dp, d).start()

    def core_copy(c, k):
        return remote(parts.at[c, k], crecv.at[c], c_ssem.at[c], c_rsem.at[c], to_core)

    def y_copy(c, d):
        return remote(
            ysend.at[c, d - 1], yrecv.at[c, d - 1], y_ssem.at[c, d - 1],
            y_rsem.at[c, d - 1], {"row": y_peer(d) * 2 + me_k},
        )

    def piece(c, dp, y, k):
        return gat.at[c, :, dp, y, k]

    def share_copy(c, dp, y, k, ssem, peer):
        ref = piece(c, dp, y, k)
        return remote(ref, ref, ssem, ag_rsem.at[c, dp, y, k], peer)

    def ag_y_copy(c, d, y):
        return share_copy(c, me_dp, y, me_k, ag_y.at[c, d - 1], {"row": y_peer(d) * 2 + me_k})

    def ag_x_copy(c, dp, y):
        return share_copy(c, dp, y, me_k, ag_x.at[c, y], to_dp)

    def ag_c_copy(c, dp, y, k):
        return share_copy(c, dp, y, k, ag_c.at[c, dp, y], to_core)

    def out_copy(c, a):
        cols = pl.ds(pl.multiple_of(c * width, width), width)
        return pltpu.make_async_copy(
            gat.at[c, a], (hid_all, gp_all)[a].at[:, :, :, :, cols], o_sem.at[c, a]
        )

    n_tile = tile_of(width, 256)
    d_tile = tile_of(depth, 256)

    def stage_a(c):
        slot = lax.rem(c, 2)

        @pl.when(c + 1 < chunks)
        def _():
            for copy in load_a(c + 1, 1 - slot):
                copy.start()

        for copy in load_a(c, slot):
            copy.wait()
        x = xg[0, me_dp].reshape(group, depth)
        dy = xg[1, me_dp].reshape(group, depth)
        for t in range(width // n_tile):
            cols = slice(t * n_tile, (t + 1) * n_tile)
            pre = jnp.dot(x, wa_in[slot, :, cols], preferred_element_type=F32)
            grad = contract_cols(dy, wa_out[slot, cols, :])
            for a, part in enumerate((pre, grad)):
                part = part.astype(BF16)
                for r in range(2 * n_y):
                    parts[c, r % 2, a, r // 2, :, cols] = part[r * share:(r + 1) * share]
        core_copy(c, other_k).start()

    def stage_b(c):
        core_copy(c, me_k).wait_recv()
        for d in range(1, n_y):
            y = y_peer(d)
            for a in range(2):
                ysend[c, d - 1, a] = (
                    parts[c, me_k, a, y].astype(F32) + crecv[c, a, y].astype(F32)
                ).astype(BF16)
            y_copy(c, d).start()

    def stage_c(c):
        for d in range(1, n_y):
            y_copy(c, d).wait_recv()
        for t in range(width // n_tile):
            cols = slice(t * n_tile, (t + 1) * n_tile)

            def total(a):
                value = parts[c, me_k, a, me_y, :, cols].astype(F32)
                value = value + crecv[c, a, me_y, :, cols].astype(F32)
                for d in range(1, n_y):
                    value = value + yrecv[c, d - 1, a, :, cols].astype(F32)
                return value

            pre, grad = total(0), total(1)
            square = pre * pre
            bend = jnp.tanh(SCALE * (pre + CUBIC * (square * pre)))
            half = 0.5 * (1.0 + bend)
            slope = half + (0.5 * pre) * (1.0 - bend * bend) * (
                SCALE * (1.0 + (3.0 * CUBIC) * square)
            )
            gat[c, 0, me_dp, me_y, me_k, :, cols] = (pre * half).astype(BF16)
            gat[c, 1, me_dp, me_y, me_k, :, cols] = (grad * slope).astype(BF16)
        for d in range(1, n_y):
            ag_y_copy(c, d, me_y).start()
        ag_x_copy(c, me_dp, me_y).start()
        ag_c_copy(c, me_dp, me_y, me_k).start()

    def stage_d(c):
        for d in range(1, n_y):
            y = y_from(d)
            ag_y_copy(c, d, y).wait_recv()
            ag_c_copy(c, me_dp, y, me_k).start()
            ag_x_copy(c, me_dp, y).start()

    def stage_e(c):
        slot = lax.rem(c, 2)

        @pl.when(c + 1 < chunks)
        def _():
            for copy in load_e(c + 1, 1 - slot):
                copy.start()

        for y in range(n_y):
            ag_c_copy(c, me_dp, y, other_k).wait_recv()
        for copy in load_e(c, slot):
            copy.wait()
        hidden = gat[c, 0, me_dp].reshape(group, width)
        grad_pre = gat[c, 1, me_dp].reshape(group, width)
        for t in range(depth // d_tile):
            cols = slice(t * d_tile, (t + 1) * d_tile)
            acc_out[:, cols] += jnp.dot(
                hidden, we_out[slot, :, cols], preferred_element_type=F32
            )
            acc_back[:, cols] += contract_cols(grad_pre, we_in[slot, cols, :])

    def stage_g(c):
        for y in range(n_y):
            ag_x_copy(c, other_dp, y).wait_recv()
            ag_c_copy(c, other_dp, y, me_k).start()

    def stage_f(c):
        for y in range(n_y):
            ag_c_copy(c, other_dp, y, other_k).wait_recv()
        for a in range(2):
            out_copy(c, a).start()

    last = 7

    def step(i, carry):
        @pl.when(i == 1)
        def _():
            for copy in load_e(0, 0):
                copy.start()

        stages = (
            (0, stage_a), (1, stage_b), (2, stage_c), (3, stage_d), (4, stage_e),
            (last - 1, stage_g), (last, stage_f),
        )
        for lag, stage in stages:
            @pl.when(jnp.logical_and(i >= lag, i < chunks + lag))
            def _(lag=lag, stage=stage):
                stage(i - lag)

        return carry

    lax.fori_loop(0, chunks + last, step, 0)

    out_ref[:, :depth] = acc_out[...].astype(BF16)
    out_ref[:, depth:] = acc_back[...].astype(BF16)
    x_out = []
    for a in range(2):
        for d in range(n_col):
            d_copy(a, other_dp, d).wait_recv()
        x_out.append(pltpu.make_async_copy(xg.at[a], (x_all, dy_all)[a], xo_sem.at[a]))
        x_out[a].start()
    for a in range(2):
        for d in range(n_col):
            d_copy(a, me_dp, d).wait_send()
        for d in range(1, n_col):
            x_copy(a, d, me_col).wait_send()

    def drain(c, carry):
        core_copy(c, other_k).wait_send()
        for d in range(1, n_y):
            y_copy(c, d).wait_send()
            ag_y_copy(c, d, me_y).wait_send()
        for y in range(n_y):
            ag_x_copy(c, me_dp, y).wait_send()
            for dp in range(2):
                ag_c_copy(c, dp, y, me_k).wait_send()
        for a in range(2):
            out_copy(c, a).wait()
        return carry

    lax.fori_loop(0, chunks, drain, 0)
    for copy in x_out:
        copy.wait()


def shards(mesh, tokens, grad_out, w_in, w_out):
    n_col, n_y = mesh.shape["col"], mesh.shape["row"] // 2
    rows, depth = tokens.shape
    hidden_units = w_in.shape[1]
    group = rows * n_col
    share = group // (2 * n_y)
    width = tile_of(hidden_units, 768)
    chunks = hidden_units // width
    dma = pltpu.SemaphoreType.DMA
    vmem, any_space = pl.BlockSpec(memory_space=pltpu.VMEM), pl.BlockSpec(memory_space=pl.ANY)
    shape = jax.ShapeDtypeStruct
    part, hid, gp, x_all, dy_all = pl.pallas_call(
        functools.partial(middle, (n_col, n_y, chunks, width)),
        out_shape=(
            shape((group, 2 * depth), BF16),
            shape((2, n_y, 2, share, hidden_units), BF16),
            shape((2, n_y, 2, share, hidden_units), BF16),
            shape((2, n_col, rows, depth), BF16),
            shape((2, n_col, rows, depth), BF16),
        ),
        in_specs=[vmem, vmem, any_space, any_space],
        out_specs=[vmem] + [any_space] * 4,
        scratch_shapes=[
            pltpu.VMEM((2, 2, n_col, rows, depth), BF16),
            pltpu.VMEM((chunks, 2, 2, n_y, share, width), BF16),
            pltpu.VMEM((chunks, 2, n_y, share, width), BF16),
            pltpu.VMEM((chunks, n_y - 1, 2, share, width), BF16),
            pltpu.VMEM((chunks, n_y - 1, 2, share, width), BF16),
            pltpu.VMEM((chunks, 2, 2, n_y, 2, share, width), BF16),
            pltpu.VMEM((2, depth, width), BF16),
            pltpu.VMEM((2, width, depth), BF16),
            pltpu.VMEM((2, depth, width), BF16),
            pltpu.VMEM((2, width, depth), BF16),
            pltpu.VMEM((group, depth), F32),
            pltpu.VMEM((group, depth), F32),
            dma((2,)),
            dma((2, n_col - 1)),
            dma((2, n_col - 1)),
            dma((2, n_col)),
            dma((2, n_col)),
            dma((chunks,)),
            dma((chunks,)),
            dma((chunks, n_y - 1)),
            dma((chunks, n_y - 1)),
            dma((chunks, 2, n_y, 2)),
            dma((chunks, n_y - 1)),
            dma((chunks, n_y)),
            dma((chunks, 2, n_y)),
            dma((2, 2)),
            dma((2, 2)),
            dma((chunks, 2)),
            dma((2,)),
        ],
        compiler_params=pltpu.CompilerParams(
            collective_id=0, has_side_effects=True, vmem_limit_bytes=60 * 2**20
        ),
        cost_estimate=pl.CostEstimate(
            flops=8 * group * depth * hidden_units,
            bytes_accessed=8 * depth * hidden_units,
            transcendentals=0,
        ),
        name="middle",
    )(tokens, grad_out, w_in, w_out)
    total = lax.psum_scatter(part, "col", scatter_dimension=0, tiled=True)
    output, grad_tokens = total[:, :depth], total[:, depth:]
    both = 2 * group
    grad_w_out = contract_rows(
        hid.reshape(both, hidden_units), dy_all.reshape(both, depth)
    ).astype(BF16)
    grad_w_in = contract_rows(
        x_all.reshape(both, depth), gp.reshape(both, hidden_units)
    ).astype(BF16)
    return output, grad_tokens, grad_w_in, grad_w_out


def solution(mesh):
    specs = (
        P(("dp", "col"), "row"),
        P(("dp", "col"), "row"),
        P("row", "col"),
        P("col", "row"),
    )
    return jax.shard_map(
        functools.partial(shards, mesh),
        mesh=mesh, in_specs=specs, out_specs=specs, check_vma=False,
    )
```

```python
import functools
import math

import jax
import jax.numpy as jnp
from jax import lax
from jax.experimental import pallas as pl
from jax.experimental.pallas import tpu as pltpu
from jax.sharding import PartitionSpec as P

MESH = pl.DeviceIdType.MESH
F32 = jnp.float32
BF16 = jnp.bfloat16
SCALE = math.sqrt(2.0 / math.pi)
CUBIC = 0.044715


def contract_rows(left, right):
    return lax.dot_general(
        left, right, (((0,), (0,)), ((), ())), preferred_element_type=F32
    )


def contract_cols(left, right):
    return lax.dot_general(
        left, right, (((1,), (1,)), ((), ())), preferred_element_type=F32
    )


def tile_of(size, largest):
    tile = largest
    while size % tile:
        tile -= 128
    return tile


def middle(
    sizes,
    x_ref, dy_ref, w_in, w_out,
    out_ref, hid_all, gp_all, x_all, dy_all,
    xg, parts, crecv, ysend, yrecv, gat, wa_in, wa_out, we_in, we_out,
    acc_out, acc_back,
    x_local, x_ssem, x_rsem, d_ssem, d_rsem,
    c_ssem, c_rsem, y_ssem, y_rsem, ag_rsem, ag_y, ag_x, ag_c,
    wa_sem, we_sem, o_sem, xo_sem,
):
    n_col, n_y, chunks, width = sizes
    rows, depth = x_ref.shape
    group = rows * n_col
    share = group // (2 * n_y)
    me_dp, me_row, me_col = (lax.axis_index(a) for a in ("dp", "row", "col"))
    me_y, me_k = me_row // 2, me_row % 2
    other_dp, other_k = 1 - me_dp, 1 - me_k

    def y_peer(d):
        return lax.rem(me_y + d, n_y)

    def y_from(d):
        return lax.rem(me_y + n_y - d, n_y)

    def col_peer(d):
        return lax.rem(me_col + d, n_col)

    def col_from(d):
        return lax.rem(me_col + n_col - d, n_col)

    def remote(src, dst, ssem, rsem, peer):
        return pltpu.make_async_remote_copy(
            src_ref=src, dst_ref=dst, send_sem=ssem, recv_sem=rsem,
            device_id=peer, device_id_type=MESH,
        )

    to_core = {"row": me_y * 2 + other_k}
    to_dp = {"dp": other_dp}

    barrier = pltpu.get_barrier_semaphore()
    peers = [to_core, to_dp]
    peers += [{"row": y_peer(d) * 2 + me_k} for d in range(1, n_y)]
    peers += [{"col": col_peer(d)} for d in range(1, n_col)]
    for peer in peers:
        pl.semaphore_signal(barrier, inc=1, device_id=peer, device_id_type=MESH)

    def load_a(c, slot):
        cols = pl.ds(pl.multiple_of(c * width, width), width)
        return (
            pltpu.make_async_copy(w_in.at[:, cols], wa_in.at[slot], wa_sem.at[slot, 0]),
            pltpu.make_async_copy(w_out.at[cols, :], wa_out.at[slot], wa_sem.at[slot, 1]),
        )

    def load_e(c, slot):
        cols = pl.ds(pl.multiple_of(c * width, width), width)
        return (
            pltpu.make_async_copy(w_in.at[:, cols], we_in.at[slot], we_sem.at[slot, 0]),
            pltpu.make_async_copy(w_out.at[cols, :], we_out.at[slot], we_sem.at[slot, 1]),
        )

    load_a(0, 0)[0].start()
    own = [
        pltpu.make_async_copy(ref, xg.at[a, me_dp, me_col], x_local.at[a])
        for a, ref in enumerate((x_ref, dy_ref))
    ]
    for copy in own:
        copy.start()
    acc_out[...] = jnp.zeros_like(acc_out)
    acc_back[...] = jnp.zeros_like(acc_back)
    pl.semaphore_wait(barrier, len(peers))

    def x_copy(a, d, at):
        ref = (x_ref, dy_ref)[a]
        return remote(
            ref, xg.at[a, me_dp, at], x_ssem.at[a, d - 1], x_rsem.at[a, d - 1],
            {"col": col_peer(d)},
        )

    for d in range(1, n_col):
        x_copy(0, d, me_col).start()
    for copy in own:
        copy.wait()

    def d_copy(a, dp, d):
        ref = xg.at[a, dp, col_from(d)]
        return remote(ref, ref, d_ssem.at[a, d], d_rsem.at[a, d], to_dp)

    for a in range(2):
        d_copy(a, me_dp, 0).start()
    def arrive(a):
        for d in range(1, n_col):
            x_copy(a, d, col_from(d)).wait_recv()
            d_copy(a, me_dp, d).start()

    arrive(0)
    for d in range(1, n_col):
        x_copy(1, d, me_col).start()

    def core_copy(c, k):
        return remote(parts.at[c, k], crecv.at[c], c_ssem.at[c], c_rsem.at[c], to_core)

    def y_copy(c, d):
        return remote(
            ysend.at[c, d - 1], yrecv.at[c, d - 1], y_ssem.at[c, d - 1],
            y_rsem.at[c, d - 1], {"row": y_peer(d) * 2 + me_k},
        )

    def piece(c, dp, y, k):
        return gat.at[c, dp, y, k]

    def share_copy(c, dp, y, k, ssem, peer):
        ref = piece(c, dp, y, k)
        return remote(ref, ref, ssem, ag_rsem.at[c, dp, y, k], peer)

    def ag_y_copy(c, d, y):
        return share_copy(c, me_dp, y, me_k, ag_y.at[c, d - 1], {"row": y_peer(d) * 2 + me_k})

    def ag_x_copy(c, dp, y):
        return share_copy(c, dp, y, me_k, ag_x.at[c, y], to_dp)

    def ag_c_copy(c, dp, y, k):
        return share_copy(c, dp, y, k, ag_c.at[c, dp, y], to_core)

    def out_copy(v, a):
        c = v - a * chunks
        cols = pl.ds(pl.multiple_of(c * width, width), width)
        return pltpu.make_async_copy(
            gat.at[v], (hid_all, gp_all)[a].at[:, :, :, :, cols], o_sem.at[v]
        )

    n_tile = tile_of(width, 256)
    d_tile = tile_of(depth, 256)

    def each(v, body):
        for a in range(2):
            @pl.when(jnp.logical_and(v >= a * chunks, v < (a + 1) * chunks))
            def _(a=a):
                body(a)

    def fetch(load, v, which):
        def body(a):
            c = v - a * chunks
            load(c, lax.rem(c, 2))[which(a)].start()

        each(v, body)

    def stage_a(c):
        fetch(load_a, c + 1, lambda a: a)

        def body(a):
            if a == 1:
                @pl.when(c == chunks)
                def _():
                    arrive(1)

            slot = lax.rem(c - a * chunks, 2)
            load_a(c - a * chunks, slot)[a].wait()
            rows_in = xg[a, me_dp].reshape(group, depth)
            for t in range(width // n_tile):
                cols = slice(t * n_tile, (t + 1) * n_tile)
                if a == 0:
                    part = jnp.dot(
                        rows_in, wa_in[slot, :, cols], preferred_element_type=F32
                    )
                else:
                    part = contract_cols(rows_in, wa_out[slot, cols, :])
                part = part.astype(BF16)
                for r in range(2 * n_y):
                    parts[c, r % 2, r // 2, :, cols] = part[r * share:(r + 1) * share]

        each(c, body)
        core_copy(c, other_k).start()

    def stage_b(c):
        core_copy(c, me_k).wait_recv()
        for d in range(1, n_y):
            y = y_peer(d)
            ysend[c, d - 1] = (
                parts[c, me_k, y].astype(F32) + crecv[c, y].astype(F32)
            ).astype(BF16)
            y_copy(c, d).start()

    def stage_c(c):
        for d in range(1, n_y):
            y_copy(c, d).wait_recv()

        def total(v, cols):
            value = parts[v, me_k, me_y, :, cols].astype(F32)
            value = value + crecv[v, me_y, :, cols].astype(F32)
            for d in range(1, n_y):
                value = value + yrecv[v, d - 1, :, cols].astype(F32)
            return value

        def body(a):
            for t in range(width // n_tile):
                cols = slice(t * n_tile, (t + 1) * n_tile)
                pre = total(c - a * chunks, cols)
                square = pre * pre
                bend = jnp.tanh(SCALE * (pre + CUBIC * (square * pre)))
                half = 0.5 * (1.0 + bend)
                value = pre * half
                if a == 1:
                    slope = half + (0.5 * pre) * (1.0 - bend * bend) * (
                        SCALE * (1.0 + (3.0 * CUBIC) * square)
                    )
                    value = total(c, cols) * slope
                gat[c, me_dp, me_y, me_k, :, cols] = value.astype(BF16)

        each(c, body)
        for d in range(1, n_y):
            ag_y_copy(c, d, me_y).start()
        ag_x_copy(c, me_dp, me_y).start()
        ag_c_copy(c, me_dp, me_y, me_k).start()

    def stage_d(c):
        for d in range(1, n_y):
            y = y_from(d)
            ag_y_copy(c, d, y).wait_recv()
            ag_c_copy(c, me_dp, y, me_k).start()
            ag_x_copy(c, me_dp, y).start()

    def stage_e(c):
        fetch(load_e, c + 1, lambda a: 1 - a)
        for y in range(n_y):
            ag_c_copy(c, me_dp, y, other_k).wait_recv()

        def body(a):
            slot = lax.rem(c - a * chunks, 2)
            load_e(c - a * chunks, slot)[1 - a].wait()
            value = gat[c, me_dp].reshape(group, width)
            for t in range(depth // d_tile):
                cols = slice(t * d_tile, (t + 1) * d_tile)
                if a == 0:
                    acc_out[:, cols] += jnp.dot(
                        value, we_out[slot, :, cols], preferred_element_type=F32
                    )
                else:
                    acc_back[:, cols] += contract_cols(value, we_in[slot, cols, :])

        each(c, body)

    def stage_g(c):
        for y in range(n_y):
            ag_x_copy(c, other_dp, y).wait_recv()
            ag_c_copy(c, other_dp, y, me_k).start()

    def stage_f(c):
        for y in range(n_y):
            ag_c_copy(c, other_dp, y, other_k).wait_recv()
        each(c, lambda a: out_copy(c, a).start())

    last = 7

    def step(i, carry):
        @pl.when(i == 1)
        def _():
            load_e(0, 0)[1].start()

        stages = (
            (0, stage_a), (1, stage_b), (2, stage_c), (3, stage_d), (4, stage_e),
            (last - 1, stage_g), (last, stage_f),
        )
        for lag, stage in stages:
            @pl.when(jnp.logical_and(i >= lag, i < 2 * chunks + lag))
            def _(lag=lag, stage=stage):
                stage(i - lag)

        return carry

    lax.fori_loop(0, 2 * chunks + last, step, 0)

    out_ref[:, :depth] = acc_out[...].astype(BF16)
    out_ref[:, depth:] = acc_back[...].astype(BF16)
    x_out = []
    for a in range(2):
        for d in range(n_col):
            d_copy(a, other_dp, d).wait_recv()
        x_out.append(pltpu.make_async_copy(xg.at[a], (x_all, dy_all)[a], xo_sem.at[a]))
        x_out[a].start()
    for a in range(2):
        for d in range(n_col):
            d_copy(a, me_dp, d).wait_send()
        for d in range(1, n_col):
            x_copy(a, d, me_col).wait_send()

    def drain(c, carry):
        core_copy(c, other_k).wait_send()
        for d in range(1, n_y):
            y_copy(c, d).wait_send()
            ag_y_copy(c, d, me_y).wait_send()
        for y in range(n_y):
            ag_x_copy(c, me_dp, y).wait_send()
            for dp in range(2):
                ag_c_copy(c, dp, y, me_k).wait_send()
        each(c, lambda a: out_copy(c, a).wait())
        return carry

    lax.fori_loop(0, 2 * chunks, drain, 0)
    for copy in x_out:
        copy.wait()


def shards(mesh, tokens, grad_out, w_in, w_out):
    n_col, n_y = mesh.shape["col"], mesh.shape["row"] // 2
    rows, depth = tokens.shape
    hidden_units = w_in.shape[1]
    group = rows * n_col
    share = group // (2 * n_y)
    width = tile_of(hidden_units, 768)
    chunks = hidden_units // width
    dma = pltpu.SemaphoreType.DMA
    vmem, any_space = pl.BlockSpec(memory_space=pltpu.VMEM), pl.BlockSpec(memory_space=pl.ANY)
    shape = jax.ShapeDtypeStruct
    part, hid, gp, x_all, dy_all = pl.pallas_call(
        functools.partial(middle, (n_col, n_y, chunks, width)),
        out_shape=(
            shape((group, 2 * depth), BF16),
            shape((2, n_y, 2, share, hidden_units), BF16),
            shape((2, n_y, 2, share, hidden_units), BF16),
            shape((2, n_col, rows, depth), BF16),
            shape((2, n_col, rows, depth), BF16),
        ),
        in_specs=[vmem, vmem, any_space, any_space],
        out_specs=[vmem] + [any_space] * 4,
        scratch_shapes=[
            pltpu.VMEM((2, 2, n_col, rows, depth), BF16),
            pltpu.VMEM((2 * chunks, 2, n_y, share, width), BF16),
            pltpu.VMEM((2 * chunks, n_y, share, width), BF16),
            pltpu.VMEM((2 * chunks, n_y - 1, share, width), BF16),
            pltpu.VMEM((2 * chunks, n_y - 1, share, width), BF16),
            pltpu.VMEM((2 * chunks, 2, n_y, 2, share, width), BF16),
            pltpu.VMEM((2, depth, width), BF16),
            pltpu.VMEM((2, width, depth), BF16),
            pltpu.VMEM((2, depth, width), BF16),
            pltpu.VMEM((2, width, depth), BF16),
            pltpu.VMEM((group, depth), F32),
            pltpu.VMEM((group, depth), F32),
            dma((2,)),
            dma((2, n_col - 1)),
            dma((2, n_col - 1)),
            dma((2, n_col)),
            dma((2, n_col)),
            dma((2 * chunks,)),
            dma((2 * chunks,)),
            dma((2 * chunks, n_y - 1)),
            dma((2 * chunks, n_y - 1)),
            dma((2 * chunks, 2, n_y, 2)),
            dma((2 * chunks, n_y - 1)),
            dma((2 * chunks, n_y)),
            dma((2 * chunks, 2, n_y)),
            dma((2, 2)),
            dma((2, 2)),
            dma((2 * chunks,)),
            dma((2,)),
        ],
        compiler_params=pltpu.CompilerParams(
            collective_id=0, has_side_effects=True, vmem_limit_bytes=60 * 2**20
        ),
        cost_estimate=pl.CostEstimate(
            flops=8 * group * depth * hidden_units,
            bytes_accessed=8 * depth * hidden_units,
            transcendentals=0,
        ),
        name="middle",
    )(tokens, grad_out, w_in, w_out)
    total = lax.psum_scatter(part, "col", scatter_dimension=0, tiled=True)
    output, grad_tokens = total[:, :depth], total[:, depth:]
    both = 2 * group
    grad_w_out = contract_rows(
        hid.reshape(both, hidden_units), dy_all.reshape(both, depth)
    ).astype(BF16)
    grad_w_in = contract_rows(
        x_all.reshape(both, depth), gp.reshape(both, hidden_units)
    ).astype(BF16)
    return output, grad_tokens, grad_w_in, grad_w_out


def solution(mesh):
    specs = (
        P(("dp", "col"), "row"),
        P(("dp", "col"), "row"),
        P("row", "col"),
        P("col", "row"),
    )
    return jax.shard_map(
        functools.partial(shards, mesh),
        mesh=mesh, in_specs=specs, out_specs=specs, check_vma=False,
    )
```
